512 devices in a mesh: row: 16 (over x_hi, z), col: 32 (over y, x_lo, core).
Axes of the slice: x: 4 (x_hi: 2, x_lo: 2; x = x_hi * 2 + x_lo), y: 8, z: 8, core: 2. Of those that a mesh axis runs over, the one named last changes fastest.
Arguments:
- points: float32 [64, 65536], P(None, ('row', 'col')), may hold values from -6 to 6
- targets: float32 [65536], P(('row', 'col')), may hold values from -6 to 6
- probes: float32 [32, 65536], P(None, ('row', 'col')), may hold values from -6 to 6
- lengthscale: float32 [1], replicated, may hold values from 3.5 to 5
- outputscale: float32 [1], replicated, may hold values from 0.5 to 2
- noise: float32 [1], replicated, may hold values from 0.05 to 0.5
Outputs:
- solution: float32 [33, 65536], P(None, ('row', 'col'))
- residual: float32 [33, 65536], P(None, ('row', 'col'))
- direction: float32 [33, 65536], P(None, ('row', 'col'))
- length_products: float32 [32, 65536], P(None, ('row', 'col'))
- scale_products: float32 [32, 65536], P(None, ('row', 'col'))
The draws below stay inside these ranges and needn't reach their ends.
All inputs are finite; a program needn't handle non-finite values.
Results may differ from the reference program's by a relative error of at most 0.0003.
Values sent between devices are 32-bit elements; how exact they have to be, the bound alone decides.
No kernel may reach another device: no remote copies, remote signals or barrier semaphores. Data moves between devices by JAX's collectives and lax.ppermute only.
A program may use at most 64 MiB of HBM per device.

```python
import math
import jax
import jax.numpy as jnp
from jax import lax

F = 64
PROBES = 32
N = 65536


def level_of(stream_key, extent, split, low, high):
    factor_of, own = 1.0, jax.random.fold_in(stream_key, 6)
    for position, shards_of in split:
        draws = jnp.exp(jax.random.uniform(jax.random.fold_in(own, position), (shards_of,), jnp.float32, low / len(split), high / len(split)))
        factor_of = factor_of * jnp.repeat(draws, extent[position] // shards_of).reshape([-1 if axis == position else 1 for axis in range(len(extent))])
    return factor_of


def scatter_about(own_key, extent, width, bound, pieces=(), kind=jnp.bfloat16):
    loudness = level_of(own_key, extent, pieces, -0.22, 0.18) if pieces else 1.0
    drawn = jax.random.normal(own_key, extent, jnp.float32) * width * loudness
    return jnp.minimum(jnp.maximum(drawn, -bound), bound).astype(kind)


def setup_inputs(seed: int = 0) -> dict:
    key_list = jax.random.split(jax.random.key(seed), 7)
    return {
        "points": scatter_about(key_list[0], (F, N), 1.0, 6.0, ((1, 512),), jnp.float32),
        "targets": scatter_about(key_list[1], (N,), 1.0, 6.0, ((0, 512),), jnp.float32),
        "probes": scatter_about(key_list[2], (PROBES, N), 1.0, 6.0, ((1, 512),), jnp.float32),
        "lengthscale": jnp.clip(jnp.exp(jax.random.uniform(key_list[3], (1,), jnp.float32, math.log(3.5), math.log(5.0))), 3.5, 5.0),
        "outputscale": jnp.clip(jnp.exp(jax.random.uniform(key_list[4], (1,), jnp.float32, math.log(0.5), math.log(2.0))), 0.5, 2.0),
        "noise": jnp.clip(jnp.exp(jax.random.uniform(key_list[5], (1,), jnp.float32, math.log(0.05), math.log(0.5))), 0.05, 0.5),
    }


def reference(points, targets, probes, lengthscale, outputscale, noise):
    rhs = jnp.concatenate([targets[None, :], probes], 0)
    inv_two = 0.5 / (lengthscale[0] * lengthscale[0])
    total = points.shape[1]
    sq_all = jnp.sum(points * points, axis=0)
    block_rows = math.gcd(total, 256)
    count = total // block_rows

    def one_block(index):
        start = (index * block_rows).astype(jnp.int32)
        x_rows = lax.dynamic_slice_in_dim(points, start, block_rows, 1)
        sq_rows = lax.dynamic_slice_in_dim(sq_all, start, block_rows, 0)
        dots = lax.dot_general(points, x_rows, (((0,), (0,)), ((), ())), precision=lax.Precision.HIGHEST, preferred_element_type=jnp.float32)
        dist = jnp.maximum(sq_all[:, None] + sq_rows[None, :] - 2.0 * dots, 0.0)
        kern = jnp.exp(-dist * inv_two)
        eb_part = jnp.dot(rhs, kern, precision=lax.Precision.HIGHEST, preferred_element_type=jnp.float32)
        ed_part = jnp.dot(probes, kern * dist, precision=lax.Precision.HIGHEST, preferred_element_type=jnp.float32)
        return eb_part, ed_part

    eb_blocks, ed_blocks = lax.map(one_block, jnp.arange(count, dtype=jnp.int32))
    eb = jnp.transpose(eb_blocks, (1, 0, 2)).reshape(rhs.shape[0], total)
    ed = jnp.transpose(ed_blocks, (1, 0, 2)).reshape(probes.shape[0], total)
    scale = outputscale[0]
    kb = scale * eb + noise[0] * rhs
    scale_products = eb[1:]
    length_products = scale / (lengthscale[0] ** 3) * ed
    norm_old = jnp.sum(rhs * rhs, axis=1)
    curv = jnp.sum(rhs * kb, axis=1)
    alpha = norm_old / curv
    solution = alpha[:, None] * rhs
    residual = rhs - alpha[:, None] * kb
    norm_new = jnp.sum(residual * residual, axis=1)
    direction = residual + (norm_new / norm_old)[:, None] * rhs
    return solution, residual, direction, length_products, scale_products
```

```python
import math

import jax
import jax.numpy as jnp
from jax import lax
from jax.experimental import pallas as pl
from jax.experimental.pallas import tpu as pltpu
from jax.sharding import Mesh, PartitionSpec as P

AXES = ("xh", "z", "y", "xl", "co")
SIZES = (2, 8, 8, 2, 2)
I_GROUP = ("y", "xl")
J_GROUP = ("xh", "z")
N_I = 16
N_J = 16
LANES = 128
F = 64
PROBES = 32
SENT = 104
BACK = 72
BI = 512
f32, bf16 = jnp.float32, jnp.bfloat16
LOG2E = math.log2(math.e)
VMEM = pl.BlockSpec(memory_space=pltpu.VMEM)
SMEM = pl.BlockSpec(memory_space=pltpu.SMEM)


def halves(x):
    hi = x.astype(bf16)
    return hi, (x - hi.astype(f32)).astype(bf16)


def tile(t, size=LANES):
    return pl.ds(pl.multiple_of(t * size, size), size)


def products_kernel(ls_ref, xi_ref, xa_ref, xb_ref, out_ref, left, sq_i, right, sq_j, rhs):
    rows = left.shape[1]
    ell = ls_ref[0]
    c = (0.5 * LOG2E) / (ell * ell)

    def prepare_i(t, unused):
        hi, lo = halves(xi_ref[t])
        x = hi.astype(f32) + lo.astype(f32)
        yh, yl = halves((2.0 * c) * x)
        at = tile(t)
        left[0:64, at] = yh
        left[64:128, at] = yl
        left[128:192, at] = yh
        left[192:256, at] = yl
        sq_i[:, at] = jnp.broadcast_to(-c * jnp.sum(x * x, axis=0, keepdims=True), (8, LANES))
        return unused

    lax.fori_loop(0, N_I, prepare_i, 0, unroll=4)

    def prepare_j(x_ref, first):
        def body(t, unused):
            hi, lo = halves(x_ref[t, 0:64])
            x = hi.astype(f32) + lo.astype(f32)
            at = tile(first + t)
            turned = jnp.concatenate([hi.astype(f32), lo.astype(f32)], axis=0).T.astype(bf16)
            right[at, 0:64] = turned[:, 0:64]
            right[at, 64:128] = turned[:, 0:64]
            right[at, 128:192] = turned[:, 64:128]
            right[at, 192:256] = turned[:, 64:128]
            sq = jnp.broadcast_to(-c * jnp.sum(x * x, axis=0, keepdims=True), (LANES, LANES))
            sq_j[at, :] = sq.T
            bh, bl = halves(x_ref[t, 64:104])
            rhs[0:40, at] = bh
            rhs[40:80, at] = bl
            return unused

        lax.fori_loop(0, N_J, body, 0, unroll=4)

    prepare_j(xa_ref, 0)
    prepare_j(xb_ref, N_J)

    def block(ib, unused):
        at = tile(ib, BI)
        dots = jnp.dot(right[...], left[:, at], preferred_element_type=f32)
        sq = jnp.concatenate([sq_j[...]] * (BI // LANES), axis=1)
        power = jnp.minimum(dots + sq_i[0:1, at] + sq, 0.0)
        kern = jnp.exp2(power)
        kh, kl = halves(kern)
        dh, dl = halves(kern * power)
        eb = jnp.dot(rhs[...], kh, preferred_element_type=f32)
        ed = jnp.dot(rhs[...], dh, preferred_element_type=f32)
        eb = eb[0:40] + eb[40:80] + jnp.dot(rhs[0:40], kl, preferred_element_type=f32)
        ed = ed[0:40] + ed[40:80] + jnp.dot(rhs[0:40], dl, preferred_element_type=f32)
        for p in range(BI // LANES):
            out_ref[ib * (BI // LANES) + p, 0:40] = eb[:, p * LANES : (p + 1) * LANES]
            out_ref[ib * (BI // LANES) + p, 40:72] = ed[0:32, p * LANES : (p + 1) * LANES]
        return unused

    lax.fori_loop(0, rows // BI, block, 0)


def products(lengthscale, xi, xa, xb):
    rows, cols = N_I * LANES, 2 * N_J * LANES
    return pl.pallas_call(
        products_kernel,
        out_shape=jax.ShapeDtypeStruct((N_I, BACK, LANES), f32),
        in_specs=[SMEM, VMEM, VMEM, VMEM],
        out_specs=VMEM,
        scratch_shapes=[
            pltpu.VMEM((256, rows), bf16),
            pltpu.VMEM((8, rows), f32),
            pltpu.VMEM((cols, 256), bf16),
            pltpu.VMEM((cols, LANES), f32),
            pltpu.VMEM((80, cols), bf16),
        ],
        compiler_params=pltpu.CompilerParams(vmem_limit_bytes=48 << 20),
        cost_estimate=pl.CostEstimate(flops=2 * rows * cols * 1024, bytes_accessed=4 << 20, transcendentals=rows * cols),
        name="products",
    )(lengthscale, xi, xa, xb)


def sums_kernel(ls_ref, os_ref, own_ref, part_ref, lp_ref, sp_ref, off_ref, stat_ref):
    total = part_ref[0]
    for s in range(1, N_I):
        total = total + part_ref[s]
    eb = total[0:40]
    sp_ref[...] = eb[0:32]
    lp_ref[...] = total[40:72] * ((-2.0 * math.log(2.0)) * os_ref[0] / ls_ref[0])
    rhs = own_ref[64:104]
    off = eb - rhs
    off_ref[...] = off
    stacked = jnp.concatenate([rhs * rhs, rhs * off, off * off, jnp.zeros((8, LANES), f32)], axis=0)
    stat_ref[...] = jnp.sum(stacked.T, axis=0, keepdims=True)


def sums(lengthscale, outputscale, own, parts):
    return pl.pallas_call(
        sums_kernel,
        out_shape=[
            jax.ShapeDtypeStruct((PROBES, LANES), f32),
            jax.ShapeDtypeStruct((PROBES, LANES), f32),
            jax.ShapeDtypeStruct((40, LANES), f32),
            jax.ShapeDtypeStruct((1, LANES), f32),
        ],
        in_specs=[SMEM, SMEM, VMEM, VMEM],
        out_specs=[VMEM] * 4,
        name="sums",
    )(lengthscale, outputscale, own, parts)


def step_kernel(os_ref, noise_ref, own_ref, off_ref, stats_ref, sol_ref, res_ref, dir_ref):
    scale, noise = os_ref[0], noise_ref[0]
    row = jnp.sum(stats_ref[...], axis=0, keepdims=True)
    column = jnp.broadcast_to(row, (LANES, LANES)).T
    rr, rg, gg = column[0:40], column[40:80], column[80:120]
    rhs, off = own_ref[64:104], off_ref[...]
    curv = (scale + noise) * rr + scale * rg
    share = scale / curv
    sol = (rr / curv) * rhs
    res = share * (rg * rhs - rr * off)
    direction = res + (share * share * (rr * gg - rg * rg)) * rhs
    for ref, value in ((sol_ref, sol), (res_ref, res), (dir_ref, direction)):
        ref[0:1] = value[32:33]
        ref[1:33] = value[0:32]


def step(outputscale, noise, own, off, stats):
    return pl.pallas_call(
        step_kernel,
        out_shape=[jax.ShapeDtypeStruct((PROBES + 1, LANES), f32)] * 3,
        in_specs=[SMEM, SMEM, VMEM, VMEM, VMEM],
        out_specs=[VMEM] * 3,
        name="step",
    )(outputscale, noise, own, off, stats)


def spread(x, axes, count):
    return lax.all_to_all(jnp.broadcast_to(x[None], (count, *x.shape)), axes, 0, 0, tiled=True)


def shards(points, targets, probes, lengthscale, outputscale, noise):
    own = jnp.concatenate([points, probes, targets[None, :], jnp.zeros((7, LANES), f32)], 0)
    xi = spread(points, I_GROUP, N_I)
    xa = spread(own, J_GROUP, N_J)
    xb = lax.ppermute(xa, "co", [(0, 1), (1, 0)])
    parts = lax.all_to_all(products(lengthscale, xi, xa, xb), I_GROUP, 0, 0, tiled=True)
    lp, sp, off, stat = sums(lengthscale, outputscale, own, parts)
    stats = spread(stat[0], AXES, 512)
    sol, res, direction = step(outputscale, noise, own, off, stats)
    return sol, res, direction, lp, sp


def solution(mesh):
    apart = Mesh(mesh.devices.reshape(SIZES), AXES)
    split = P(None, AXES)
    return jax.shard_map(
        shards,
        mesh=apart,
        in_specs=(split, P(AXES), split, P(), P(), P()),
        out_specs=(split,) * 5,
        check_vma=False,
    )
```

```python
import math

import jax
import jax.numpy as jnp
from jax import lax
from jax.experimental import pallas as pl
from jax.experimental.pallas import tpu as pltpu
from jax.sharding import Mesh, PartitionSpec as P

AXES = ("xh", "zh", "zm", "za", "yb", "ya", "xl", "co")
SIZES = (2, 2, 2, 2, 4, 2, 2, 2)
I_GROUP = ("ya", "za", "xh", "xl")
J_GROUP = ("yb", "zh", "zm")
SUM_FIRST = ("yb", "ya", "co")
SUM_LAST = ("xh", "xl", "zh", "zm", "za")
N_I = 16
N_J = 16
N_FIRST = 16
N_LAST = 32
LANES = 128
F = 64
PROBES = 32
RHS = 40
SENT = F + RHS
BACK = RHS + PROBES
HALF = 48
BI = 256
UNROLL = 8
PRODUCTS_MIB = 32
f32, bf16 = jnp.float32, jnp.bfloat16
LOG2E = math.log2(math.e)
VMEM = pl.BlockSpec(memory_space=pltpu.VMEM)
SMEM = pl.BlockSpec(memory_space=pltpu.SMEM)


def small(mib=8):
    return pltpu.CompilerParams(vmem_limit_bytes=mib << 20)


def shaped(*shape, dtype=f32):
    return jax.ShapeDtypeStruct(shape, dtype)


def halves(x):
    hi = x.astype(bf16)
    return hi, (x - hi.astype(f32)).astype(bf16)


def tile(t, size=LANES):
    return pl.ds(pl.multiple_of(t * size, size), size)


def rate(ls_ref):
    ell = ls_ref[0]
    return (0.5 * LOG2E) / (ell * ell)


def pack_kernel(points_ref, probes_ref, targets_ref, to_j_ref, rhs_ref):
    x = points_ref[...]
    rhs_ref[0:32] = probes_ref[...]
    rhs_ref[32:40] = jnp.concatenate([targets_ref[...], jnp.zeros((7, LANES), f32)], axis=0)
    rhs = rhs_ref[...]
    for t in range(N_J):
        to_j_ref[t, 0:F] = x
        to_j_ref[t, F:SENT] = rhs


def pack(points, probes, targets):
    return pl.pallas_call(
        pack_kernel,
        out_shape=[shaped(N_J, SENT, LANES), shaped(RHS, LANES)],
        in_specs=[VMEM] * 3,
        out_specs=[VMEM] * 2,
        compiler_params=small(60),
        cost_estimate=pl.CostEstimate(flops=0, bytes_accessed=2 << 20, transcendentals=0),
        name="pack",
    )(points, probes, targets[None, :])


def products_kernel(ls_ref, me_ref, *refs):
    xi_refs, xj_ref, acc_refs, (out_ref, left, sq_i, right, sq_j, rhs) = refs[:5], refs[5], refs[6:-6], refs[-6:]
    c = rate(ls_ref)

    def prepare_j(t, unused):
        hi, lo = halves(xj_ref[t, 0:F])
        x = hi.astype(f32) + lo.astype(f32)
        at = tile(t)
        turned = jnp.concatenate([hi.astype(f32), lo.astype(f32)], axis=0).T.astype(bf16)
        right[at, 0:64] = turned[:, 0:64]
        right[at, 64:128] = turned[:, 0:64]
        right[at, 128:192] = turned[:, 64:128]
        right[at, 192:256] = turned[:, 64:128]
        sq = jnp.broadcast_to(-c * jnp.sum(x * x, axis=0, keepdims=True), (LANES, LANES))
        sq_j[at, :] = sq.T
        b = jnp.concatenate([xj_ref[t, F:SENT], jnp.zeros((HALF - RHS, LANES), f32)], axis=0)
        bh, bl = halves(b)
        rhs[0:HALF, at] = bh
        rhs[HALF : 2 * HALF, at] = bl
        return unused

    lax.fori_loop(0, N_J, prepare_j, 0, unroll=True)

    def prepare_i(points, place):
        hi, lo = halves(points)
        x = hi.astype(f32) + lo.astype(f32)
        yh, yl = halves((2.0 * c) * x)
        at = tile(jnp.bitwise_xor(place, me_ref[0]))
        left[0:64, at] = yh
        left[64:128, at] = yl
        left[128:192, at] = yh
        left[192:256, at] = yl
        sq_i[:, at] = jnp.broadcast_to(-c * jnp.sum(x * x, axis=0, keepdims=True), (8, LANES))

    prepare_i(xi_refs[0][...], 0)
    for s in range(4):
        for t in range(1 << s):
            prepare_i(xi_refs[1 + s][t], (1 << s) + t)

    def block(ib, unused):
        at = tile(ib, BI)
        dots = jnp.dot(right[...], left[:, at], preferred_element_type=f32)
        sq = jnp.concatenate([sq_j[...]] * (BI // LANES), axis=1)
        power = jnp.minimum(dots + sq_i[0:1, at] + sq, 0.0)
        kern = jnp.exp2(power)
        kh, kl = halves(kern)
        dh, dl = halves(kern * power)
        b, d, bl, dl = (jnp.dot(rhs[...], m, preferred_element_type=f32) for m in (kh, dh, kl, dl))
        b, d = b + bl, d + dl
        b = b[0:RHS] + b[HALF : HALF + RHS]
        d = d[0:PROBES] + d[HALF : HALF + PROBES]
        both = jnp.concatenate([b, d], axis=0)
        for p in range(BI // LANES):
            t = ib * (BI // LANES) + p
            part = both[:, p * LANES : (p + 1) * LANES]
            out_ref[t] = acc_refs[0][t] + part if acc_refs else part
        return unused

    lax.fori_loop(0, N_I * LANES // BI, block, 0, unroll=UNROLL)


def products(lengthscale, me, xi, xj, *acc):
    rows, cols = N_I * LANES, N_J * LANES
    return pl.pallas_call(
        products_kernel,
        out_shape=shaped(N_I, BACK, LANES),
        in_specs=[SMEM] * 2 + [VMEM] * (6 + len(acc)),
        out_specs=VMEM,
        scratch_shapes=[
            pltpu.VMEM((256, rows), bf16),
            pltpu.VMEM((8, rows), f32),
            pltpu.VMEM((cols, 256), bf16),
            pltpu.VMEM((cols, LANES), f32),
            pltpu.VMEM((2 * HALF, cols), bf16),
        ],
        compiler_params=small(PRODUCTS_MIB),
        cost_estimate=pl.CostEstimate(flops=2 * rows * cols * 1280, bytes_accessed=2 << 20, transcendentals=rows * cols),
        name="products",
    )(lengthscale, me, *xi, xj, *acc)


def sums_kernel(ls_ref, os_ref, rhs_ref, part_ref, lp_ref, sp_ref, off_ref, stat_ref):
    total = part_ref[0]
    for s in range(1, N_I):
        total = total + part_ref[s]
    eb = total[0:RHS]
    sp_ref[...] = eb[0:PROBES]
    lp_ref[...] = total[RHS:BACK] * ((-2.0 * math.log(2.0)) * os_ref[0] / ls_ref[0])
    rhs = rhs_ref[...]
    off = eb - rhs
    off_ref[...] = off
    stacked = jnp.concatenate([rhs * rhs, rhs * off, off * off, jnp.zeros((8, LANES), f32)], axis=0)
    stat_ref[...] = jnp.broadcast_to(jnp.sum(stacked.T, axis=0, keepdims=True), (N_FIRST, LANES))


def sums(lengthscale, outputscale, rhs, parts):
    return pl.pallas_call(
        sums_kernel,
        out_shape=[shaped(PROBES, LANES), shaped(PROBES, LANES), shaped(RHS, LANES), shaped(N_FIRST, LANES)],
        in_specs=[SMEM, SMEM, VMEM, VMEM],
        out_specs=[VMEM] * 4,
        compiler_params=small(),
        name="sums",
    )(lengthscale, outputscale, rhs, parts)


def again_kernel(stats_ref, out_ref):
    out_ref[...] = jnp.broadcast_to(jnp.sum(stats_ref[...], axis=0, keepdims=True), (N_LAST, LANES))


def again(stats):
    return pl.pallas_call(
        again_kernel, out_shape=shaped(N_LAST, LANES), in_specs=[VMEM], out_specs=VMEM, compiler_params=small(), name="again"
    )(stats)


def step_kernel(os_ref, noise_ref, rhs_ref, off_ref, stats_ref, sol_ref, res_ref, dir_ref):
    scale, noise = os_ref[0], noise_ref[0]
    row = jnp.sum(stats_ref[...], axis=0, keepdims=True)
    column = jnp.broadcast_to(row, (LANES, LANES)).T
    rr, rg, gg = column[0:RHS], column[RHS : 2 * RHS], column[2 * RHS : 3 * RHS]
    rhs, off = rhs_ref[...], off_ref[...]
    curv = (scale + noise) * rr + scale * rg
    share = scale / curv
    sol = (rr / curv) * rhs
    res = share * (rg * rhs - rr * off)
    direction = res + (share * share * (rr * gg - rg * rg)) * rhs
    for ref, value in ((sol_ref, sol), (res_ref, res), (dir_ref, direction)):
        ref[0:1] = value[32:33]
        ref[1:33] = value[0:32]


def step(outputscale, noise, rhs, off, stats):
    return pl.pallas_call(
        step_kernel,
        out_shape=[shaped(PROBES + 1, LANES)] * 3,
        in_specs=[SMEM, SMEM, VMEM, VMEM, VMEM],
        out_specs=[VMEM] * 3,
        compiler_params=small(),
        name="step",
    )(outputscale, noise, rhs, off, stats)


def exchange(x, axes):
    return lax.all_to_all(x, axes, 0, 0, tiled=True)


def swap(x, axis):
    return lax.ppermute(x, axis, [(0, 1), (1, 0)])


def shards(points, targets, probes, lengthscale, outputscale, noise):
    to_j, rhs = pack(points, probes, targets)
    xa = exchange(to_j, J_GROUP)
    pieces, held = [points], points[None]
    for axis in reversed(I_GROUP):
        pieces.append(swap(held, axis))
        held = jnp.concatenate([held, pieces[-1]], axis=0)
    xb = swap(xa, "co")
    me = lax.axis_index(I_GROUP).reshape(1)
    half = products(lengthscale, me, pieces, xa)
    parts = exchange(products(lengthscale, me, pieces, xb, half), I_GROUP)
    lp, sp, off, stat = sums(lengthscale, outputscale, rhs, parts)
    stats = exchange(again(exchange(stat, SUM_FIRST)), SUM_LAST)
    sol, res, direction = step(outputscale, noise, rhs, off, stats)
    return sol, res, direction, lp, sp


def solution(mesh):
    apart = Mesh(mesh.devices.reshape(SIZES), AXES)
    split = P(None, AXES)
    return jax.shard_map(
        shards,
        mesh=apart,
        in_specs=(split, P(AXES), split, P(), P(), P()),
        out_specs=(split,) * 5,
        check_vma=False,
    )
```

```python
import math

import jax
import jax.numpy as jnp
from jax import lax
from jax.experimental import pallas as pl
from jax.experimental.pallas import tpu as pltpu
from jax.sharding import Mesh, PartitionSpec as P

AXES = ("xh", "zh", "zm", "za", "yb", "ya", "xl", "co")
SIZES = (2, 2, 2, 2, 4, 2, 2, 2)
I_GROUP = ("za", "ya", "xh", "xl")
J_GROUP = ("yb", "zh", "zm")
SUM_FIRST = ("yb", "ya", "co")
SUM_LAST = ("xh", "xl", "zh", "zm", "za")
N_I = 16
N_J = 16
N_FIRST = 16
N_LAST = 32
LANES = 128
F = 64
PROBES = 32
RHS = 40
SENT = F + RHS
BACK = RHS + PROBES
HALF = 48
BI = 256
PRODUCTS_MIB = 32
f32, bf16 = jnp.float32, jnp.bfloat16
LOG2E = math.log2(math.e)
VMEM = pl.BlockSpec(memory_space=pltpu.VMEM)
SMEM = pl.BlockSpec(memory_space=pltpu.SMEM)


def small(mib=8):
    return pltpu.CompilerParams(vmem_limit_bytes=mib << 20)


def shaped(*shape, dtype=f32):
    return jax.ShapeDtypeStruct(shape, dtype)


def halves(x):
    hi = x.astype(bf16)
    return hi, (x - hi.astype(f32)).astype(bf16)


def tile(t, size=LANES):
    return pl.ds(pl.multiple_of(t * size, size), size)


def pack_kernel(points_ref, probes_ref, targets_ref, to_j_ref, rhs_ref):
    x = points_ref[...]
    rhs_ref[0:32] = probes_ref[...]
    rhs_ref[32:40] = jnp.concatenate([targets_ref[...], jnp.zeros((7, LANES), f32)], axis=0)
    rhs = rhs_ref[...]
    for t in range(N_J):
        to_j_ref[t, 0:F] = x
        to_j_ref[t, F:SENT] = rhs


def pack(points, probes, targets):
    return pl.pallas_call(
        pack_kernel,
        out_shape=[shaped(N_J, SENT, LANES), shaped(RHS, LANES)],
        in_specs=[VMEM] * 3,
        out_specs=[VMEM] * 2,
        compiler_params=small(60),
        cost_estimate=pl.CostEstimate(flops=0, bytes_accessed=2 << 20, transcendentals=0),
        name="pack",
    )(points, probes, targets[None, :])


def prepare_j(c, xj_ref, right, sq_j, rhs):
    for t in range(N_J):
        hi, lo = halves(xj_ref[t, 0:F])
        x = hi.astype(f32) + lo.astype(f32)
        at = slice(t * LANES, (t + 1) * LANES)
        turned = jnp.concatenate([hi.astype(f32), lo.astype(f32)], axis=0).T.astype(bf16)
        right[at, 0:64] = turned[:, 0:64]
        right[at, 64:128] = turned[:, 0:64]
        right[at, 128:192] = turned[:, 64:128]
        right[at, 192:256] = turned[:, 64:128]
        sq = jnp.broadcast_to(-c * jnp.sum(x * x, axis=0, keepdims=True), (LANES, LANES))
        sq_j[at, :] = sq.T
        b = jnp.concatenate([xj_ref[t, F:SENT], jnp.zeros((HALF - RHS, LANES), f32)], axis=0)
        bh, bl = halves(b)
        rhs[0:HALF, at] = bh
        rhs[HALF : 2 * HALF, at] = bl


def blocks(left, sq_i, right, sq_j, rhs, acc_ref, out_ref):
    for ib in range(N_I * LANES // BI):
        at = slice(ib * BI, (ib + 1) * BI)
        dots = jnp.dot(right[...], left[:, at], preferred_element_type=f32)
        sq = jnp.concatenate([sq_j[...]] * (BI // LANES), axis=1)
        power = jnp.minimum(dots + sq_i[0:1, at] + sq, 0.0)
        kern = jnp.exp2(power)
        kh, kl = halves(kern)
        dh, dl = halves(kern * power)
        b, d, bl, dl = (jnp.dot(rhs[...], m, preferred_element_type=f32) for m in (kh, dh, kl, dl))
        b, d = b + bl, d + dl
        b = b[0:RHS] + b[HALF : HALF + RHS]
        d = d[0:PROBES] + d[HALF : HALF + PROBES]
        both = jnp.concatenate([b, d], axis=0)
        for p in range(BI // LANES):
            t = ib * (BI // LANES) + p
            part = both[:, p * LANES : (p + 1) * LANES]
            out_ref[t] = part if acc_ref is None else acc_ref[t] + part


def first_kernel(ls_ref, os_ref, noise_ref, me_ref, *refs):
    xi_refs, xj_ref, (out_ref, left, sq_i, params_ref), scratch = refs[:4], refs[4], refs[5:9], refs[9:]
    ell = ls_ref[0]
    c = (0.5 * LOG2E) / (ell * ell)
    for row, value in enumerate((c, os_ref[0], noise_ref[0], (-2.0 * math.log(2.0)) * os_ref[0] / ell)):
        params_ref[row : row + 1] = jnp.full((1, LANES), value, f32)
    prepare_j(c, xj_ref, *scratch)
    for s in range(4):
        for t in range(4):
            hi, lo = halves(xi_refs[s][t])
            x = hi.astype(f32) + lo.astype(f32)
            yh, yl = halves((2.0 * c) * x)
            at = tile(jnp.bitwise_xor(4 * s + t, me_ref[0]))
            left[0:64, at] = yh
            left[64:128, at] = yl
            left[128:192, at] = yh
            left[192:256, at] = yl
            sq_i[:, at] = jnp.broadcast_to(-c * jnp.sum(x * x, axis=0, keepdims=True), (8, LANES))
    blocks(left, sq_i, *scratch, None, out_ref)


def second_kernel(acc_ref, left, sq_i, params_ref, xj_ref, out_ref, *scratch):
    prepare_j(params_ref[0:1], xj_ref, *scratch)
    blocks(left, sq_i, *scratch, acc_ref, out_ref)


def products_call(kernel, out_shape, in_specs, out_specs, name):
    rows, cols = N_I * LANES, N_J * LANES
    return pl.pallas_call(
        kernel,
        out_shape=out_shape,
        in_specs=in_specs,
        out_specs=out_specs,
        scratch_shapes=[
            pltpu.VMEM((cols, 256), bf16),
            pltpu.VMEM((cols, LANES), f32),
            pltpu.VMEM((2 * HALF, cols), bf16),
        ],
        compiler_params=small(PRODUCTS_MIB),
        cost_estimate=pl.CostEstimate(flops=2 * rows * cols * 1280, bytes_accessed=2 << 20, transcendentals=rows * cols),
        name=name,
    )


def first_products(lengthscale, outputscale, noise, me, pieces, xj):
    rows = N_I * LANES
    out_shape = [shaped(N_I, BACK, LANES), shaped(256, rows, dtype=bf16), shaped(8, rows), shaped(8, LANES)]
    call = products_call(first_kernel, out_shape, [SMEM] * 4 + [VMEM] * 5, [VMEM] * 4, "first_products")
    return call(lengthscale, outputscale, noise, me, *pieces, xj)


def second_products(acc, left, sq_i, params, xj):
    call = products_call(second_kernel, shaped(N_I, BACK, LANES), [VMEM] * 5, VMEM, "second_products")
    return call(acc, left, sq_i, params, xj)


def sums_kernel(params_ref, rhs_ref, part_ref, lp_ref, sp_ref, off_ref, stat_ref):
    total = part_ref[0]
    for s in range(1, N_I):
        total = total + part_ref[s]
    eb = total[0:RHS]
    sp_ref[...] = eb[0:PROBES]
    lp_ref[...] = total[RHS:BACK] * params_ref[3:4]
    rhs = rhs_ref[...]
    off = eb - rhs
    off_ref[...] = off
    stacked = jnp.concatenate([rhs * rhs, rhs * off, off * off, jnp.zeros((8, LANES), f32)], axis=0)
    stat_ref[...] = jnp.broadcast_to(jnp.sum(stacked.T, axis=0, keepdims=True), (N_FIRST, LANES))


def sums(params, rhs, parts):
    return pl.pallas_call(
        sums_kernel,
        out_shape=[shaped(PROBES, LANES), shaped(PROBES, LANES), shaped(RHS, LANES), shaped(N_FIRST, LANES)],
        in_specs=[VMEM] * 3,
        out_specs=[VMEM] * 4,
        compiler_params=small(),
        name="sums",
    )(params, rhs, parts)


def again_kernel(stats_ref, out_ref):
    out_ref[...] = jnp.broadcast_to(jnp.sum(stats_ref[...], axis=0, keepdims=True), (N_LAST, LANES))


def again(stats):
    return pl.pallas_call(
        again_kernel, out_shape=shaped(N_LAST, LANES), in_specs=[VMEM], out_specs=VMEM, compiler_params=small(), name="again"
    )(stats)


def step_kernel(params_ref, rhs_ref, off_ref, stats_ref, sol_ref, res_ref, dir_ref):
    scale, noise = params_ref[1:2], params_ref[2:3]
    row = jnp.sum(stats_ref[...], axis=0, keepdims=True)
    column = jnp.broadcast_to(row, (LANES, LANES)).T
    rr, rg, gg = column[0:RHS], column[RHS : 2 * RHS], column[2 * RHS : 3 * RHS]
    rhs, off = rhs_ref[...], off_ref[...]
    curv = (scale + noise) * rr + scale * rg
    share = scale / curv
    sol = (rr / curv) * rhs
    res = share * (rg * rhs - rr * off)
    direction = res + (share * share * (rr * gg - rg * rg)) * rhs
    for ref, value in ((sol_ref, sol), (res_ref, res), (dir_ref, direction)):
        ref[0:1] = value[32:33]
        ref[1:33] = value[0:32]


def step(params, rhs, off, stats):
    return pl.pallas_call(
        step_kernel,
        out_shape=[shaped(PROBES + 1, LANES)] * 3,
        in_specs=[VMEM] * 4,
        out_specs=[VMEM] * 3,
        compiler_params=small(),
        name="step",
    )(params, rhs, off, stats)


def exchange(x, axes):
    return lax.all_to_all(x, axes, 0, 0, tiled=True)


def swap(x, axis):
    return lax.ppermute(x, axis, [(0, 1), (1, 0)])


def others(x, axes):
    return [lax.ppermute(x, axes, [(i, i ^ m) for i in range(4)]) for m in (1, 2, 3)]


def shards(points, targets, probes, lengthscale, outputscale, noise):
    to_j, rhs = pack(points, probes, targets)
    xa = exchange(to_j, J_GROUP)
    near = jnp.stack([points] + others(points, I_GROUP[2:]))
    pieces = [near] + others(near, I_GROUP[:2])
    xb = swap(xa, "co")
    me = lax.axis_index(I_GROUP).reshape(1)
    half, left, sq_i, params = first_products(lengthscale, outputscale, noise, me, pieces, xa)
    parts = exchange(second_products(half, left, sq_i, params, xb), I_GROUP)
    lp, sp, off, stat = sums(params, rhs, parts)
    stats = exchange(again(exchange(stat, SUM_FIRST)), SUM_LAST)
    sol, res, direction = step(params, rhs, off, stats)
    return sol, res, direction, lp, sp


def solution(mesh):
    apart = Mesh(mesh.devices.reshape(SIZES), AXES)
    split = P(None, AXES)
    return jax.shard_map(
        shards,
        mesh=apart,
        in_specs=(split, P(AXES), split, P(), P(), P()),
        out_specs=(split,) * 5,
        check_vma=False,
    )
```

```python
import math

import jax
import jax.numpy as jnp
from jax import lax
from jax.experimental import pallas as pl
from jax.experimental.pallas import tpu as pltpu
from jax.sharding import Mesh, PartitionSpec as P

AXES = ("xh", "zh", "zm", "za", "yb", "ya", "xl", "co")
SIZES = (2, 2, 2, 2, 4, 2, 2, 2)
I_GROUP = ("za", "ya", "xh", "xl")
J_GROUP = ("zh", "zm", "yb")
SUM_FIRST = ("yb", "ya", "co")
SUM_LAST = ("xh", "xl", "zh", "zm", "za")
N_I = 16
N_J = 16
N_FIRST = 16
N_LAST = 32
LANES = 128
F = 64
PROBES = 32
RHS = 40
SENT = F + RHS
BACK = RHS + PROBES
HALF = 48
BI = 256
PRODUCTS_MIB = 32
f32, bf16 = jnp.float32, jnp.bfloat16
LOG2E = math.log2(math.e)
VMEM = pl.BlockSpec(memory_space=pltpu.VMEM)
SMEM = pl.BlockSpec(memory_space=pltpu.SMEM)


def small(mib=8):
    return pltpu.CompilerParams(vmem_limit_bytes=mib << 20)


def shaped(*shape, dtype=f32):
    return jax.ShapeDtypeStruct(shape, dtype)


def halves(x):
    hi = x.astype(bf16)
    return hi, (x - hi.astype(f32)).astype(bf16)


def tile(t, size=LANES):
    return pl.ds(pl.multiple_of(t * size, size), size)


def pack_kernel(points_ref, probes_ref, targets_ref, to_j_ref, rhs_ref):
    x = points_ref[...]
    rhs_ref[0:32] = probes_ref[...]
    rhs_ref[32:40] = jnp.concatenate([targets_ref[...], jnp.zeros((7, LANES), f32)], axis=0)
    rhs = rhs_ref[...]
    for t in range(N_J):
        to_j_ref[t, 0:F] = x
        to_j_ref[t, F:SENT] = rhs


def pack(points, probes, targets):
    return pl.pallas_call(
        pack_kernel,
        out_shape=[shaped(N_J, SENT, LANES), shaped(RHS, LANES)],
        in_specs=[VMEM] * 3,
        out_specs=[VMEM] * 2,
        compiler_params=small(60),
        cost_estimate=pl.CostEstimate(flops=0, bytes_accessed=2 << 20, transcendentals=0),
        name="pack",
    )(points, probes, targets[None, :])


def prepare_j(c, xj_ref, right, sq_j, rhs):
    for t in range(N_J):
        hi, lo = halves(xj_ref[t, 0:F])
        x = hi.astype(f32) + lo.astype(f32)
        at = slice(t * LANES, (t + 1) * LANES)
        turned = jnp.concatenate([hi.astype(f32), lo.astype(f32)], axis=0).T.astype(bf16)
        right[at, 0:64] = turned[:, 0:64]
        right[at, 64:128] = turned[:, 0:64]
        right[at, 128:192] = turned[:, 64:128]
        right[at, 192:256] = turned[:, 64:128]
        sq = jnp.broadcast_to(-c * jnp.sum(x * x, axis=0, keepdims=True), (LANES, LANES))
        sq_j[at, :] = sq.T
        b = jnp.concatenate([xj_ref[t, F:SENT], jnp.zeros((HALF - RHS, LANES), f32)], axis=0)
        bh, bl = halves(b)
        rhs[0:HALF, at] = bh
        rhs[HALF : 2 * HALF, at] = bl


def blocks(left, sq_i, right, sq_j, rhs, acc_ref, out_ref):
    for ib in range(N_I * LANES // BI):
        at = slice(ib * BI, (ib + 1) * BI)
        dots = jnp.dot(right[...], left[:, at], preferred_element_type=f32)
        sq = jnp.concatenate([sq_j[...]] * (BI // LANES), axis=1)
        power = jnp.minimum(dots + sq_i[0:1, at] + sq, 0.0)
        kern = jnp.exp2(power)
        kh, kl = halves(kern)
        dh, dl = halves(kern * power)
        b, d, bl, dl = (jnp.dot(rhs[...], m, preferred_element_type=f32) for m in (kh, dh, kl, dl))
        b, d = b + bl, d + dl
        b = b[0:RHS] + b[HALF : HALF + RHS]
        d = d[0:PROBES] + d[HALF : HALF + PROBES]
        both = jnp.concatenate([b, d], axis=0)
        for p in range(BI // LANES):
            t = ib * (BI // LANES) + p
            part = both[:, p * LANES : (p + 1) * LANES]
            out_ref[t] = part if acc_ref is None else acc_ref[t] + part


def first_kernel(ls_ref, os_ref, noise_ref, me_ref, *refs):
    xi_refs, xj_ref, (out_ref, left, sq_i, params_ref), scratch = refs[:4], refs[4], refs[5:9], refs[9:]
    ell = ls_ref[0]
    c = (0.5 * LOG2E) / (ell * ell)
    for row, value in enumerate((c, os_ref[0], noise_ref[0], (-2.0 * math.log(2.0)) * os_ref[0] / ell)):
        params_ref[row : row + 1] = jnp.full((1, LANES), value, f32)
    prepare_j(c, xj_ref, *scratch)
    for s in range(4):
        for t in range(4):
            hi, lo = halves(xi_refs[s][t])
            x = hi.astype(f32) + lo.astype(f32)
            yh, yl = halves((2.0 * c) * x)
            at = tile(jnp.bitwise_xor(4 * s + t, me_ref[0]))
            left[0:64, at] = yh
            left[64:128, at] = yl
            left[128:192, at] = yh
            left[192:256, at] = yl
            sq_i[:, at] = jnp.broadcast_to(-c * jnp.sum(x * x, axis=0, keepdims=True), (8, LANES))
    blocks(left, sq_i, *scratch, None, out_ref)


def second_kernel(acc_ref, left, sq_i, params_ref, xj_ref, out_ref, *scratch):
    prepare_j(params_ref[0:1], xj_ref, *scratch)
    blocks(left, sq_i, *scratch, acc_ref, out_ref)


def products_call(kernel, out_shape, in_specs, out_specs, name):
    rows, cols = N_I * LANES, N_J * LANES
    return pl.pallas_call(
        kernel,
        out_shape=out_shape,
        in_specs=in_specs,
        out_specs=out_specs,
        scratch_shapes=[
            pltpu.VMEM((cols, 256), bf16),
            pltpu.VMEM((cols, LANES), f32),
            pltpu.VMEM((2 * HALF, cols), bf16),
        ],
        compiler_params=small(PRODUCTS_MIB),
        cost_estimate=pl.CostEstimate(flops=2 * rows * cols * 1280, bytes_accessed=2 << 20, transcendentals=rows * cols),
        name=name,
    )


def first_products(lengthscale, outputscale, noise, me, pieces, xj):
    rows = N_I * LANES
    out_shape = [shaped(N_I, BACK, LANES), shaped(256, rows, dtype=bf16), shaped(8, rows), shaped(8, LANES)]
    call = products_call(first_kernel, out_shape, [SMEM] * 4 + [VMEM] * 5, [VMEM] * 4, "first_products")
    return call(lengthscale, outputscale, noise, me, *pieces, xj)


def second_products(acc, left, sq_i, params, xj):
    call = products_call(second_kernel, shaped(N_I, BACK, LANES), [VMEM] * 5, VMEM, "second_products")
    return call(acc, left, sq_i, params, xj)


def sums_kernel(params_ref, rhs_ref, part_ref, lp_ref, sp_ref, off_ref, stat_ref):
    total = part_ref[0]
    for s in range(1, N_I):
        total = total + part_ref[s]
    eb = total[0:RHS]
    sp_ref[...] = eb[0:PROBES]
    lp_ref[...] = total[RHS:BACK] * params_ref[3:4]
    rhs = rhs_ref[...]
    off = eb - rhs
    off_ref[...] = off
    stacked = jnp.concatenate([rhs * rhs, rhs * off, off * off, jnp.zeros((8, LANES), f32)], axis=0)
    stat_ref[...] = jnp.broadcast_to(jnp.sum(stacked.T, axis=0, keepdims=True), (N_FIRST, LANES))


def sums(params, rhs, parts):
    return pl.pallas_call(
        sums_kernel,
        out_shape=[shaped(PROBES, LANES), shaped(PROBES, LANES), shaped(RHS, LANES), shaped(N_FIRST, LANES)],
        in_specs=[VMEM] * 3,
        out_specs=[VMEM] * 4,
        compiler_params=small(),
        name="sums",
    )(params, rhs, parts)


def again_kernel(stats_ref, out_ref):
    out_ref[...] = jnp.broadcast_to(jnp.sum(stats_ref[...], axis=0, keepdims=True), (N_LAST, LANES))


def again(stats):
    return pl.pallas_call(
        again_kernel, out_shape=shaped(N_LAST, LANES), in_specs=[VMEM], out_specs=VMEM, compiler_params=small(), name="again"
    )(stats)


def step_kernel(params_ref, rhs_ref, off_ref, stats_ref, sol_ref, res_ref, dir_ref):
    scale, noise = params_ref[1:2], params_ref[2:3]
    row = jnp.sum(stats_ref[...], axis=0, keepdims=True)
    column = jnp.broadcast_to(row, (LANES, LANES)).T
    rr, rg, gg = column[0:RHS], column[RHS : 2 * RHS], column[2 * RHS : 3 * RHS]
    rhs, off = rhs_ref[...], off_ref[...]
    curv = (scale + noise) * rr + scale * rg
    share = scale / curv
    sol = (rr / curv) * rhs
    res = share * (rg * rhs - rr * off)
    direction = res + (share * share * (rr * gg - rg * rg)) * rhs
    for ref, value in ((sol_ref, sol), (res_ref, res), (dir_ref, direction)):
        ref[0:1] = value[32:33]
        ref[1:33] = value[0:32]


def step(params, rhs, off, stats):
    return pl.pallas_call(
        step_kernel,
        out_shape=[shaped(PROBES + 1, LANES)] * 3,
        in_specs=[VMEM] * 4,
        out_specs=[VMEM] * 3,
        compiler_params=small(),
        name="step",
    )(params, rhs, off, stats)


def exchange(x, axes):
    return lax.all_to_all(x, axes, 0, 0, tiled=True)


def swap(x, axis):
    return lax.ppermute(x, axis, [(0, 1), (1, 0)])


def others(x, axes):
    return [lax.ppermute(x, axes, [(i, i ^ m) for i in range(4)]) for m in (1, 2, 3)]


def shards(points, targets, probes, lengthscale, outputscale, noise):
    to_j, rhs = pack(points, probes, targets)
    xa = exchange(to_j, J_GROUP)
    near = jnp.stack([points] + others(points, I_GROUP[2:]))
    pieces = [near] + others(near, I_GROUP[:2])
    xb = swap(xa, "co")
    me = lax.axis_index(I_GROUP).reshape(1)
    half, left, sq_i, params = first_products(lengthscale, outputscale, noise, me, pieces, xa)
    parts = exchange(second_products(half, left, sq_i, params, xb), I_GROUP)
    lp, sp, off, stat = sums(params, rhs, parts)
    stats = exchange(again(exchange(stat, SUM_FIRST)), SUM_LAST)
    sol, res, direction = step(params, rhs, off, stats)
    return sol, res, direction, lp, sp


def solution(mesh):
    apart = Mesh(mesh.devices.reshape(SIZES), AXES)
    split = P(None, AXES)
    return jax.shard_map(
        shards,
        mesh=apart,
        in_specs=(split, P(AXES), split, P(), P(), P()),
        out_specs=(split,) * 5,
        check_vma=False,
    )
```
